32 devices in a mesh: seq: 8 (over y, x, core), exp: 4 (over z).
Axes of the slice: x: 2, y: 2, z: 4, core: 2. Of those that a mesh axis runs over, the one named last changes fastest.
Arguments:
- tokens: bfloat16 [1536, 3584], P('exp', 'seq'), may hold values from -6 to 6
- routes: int32 [1536, 2], P('exp'), may hold values from 0 to 3, all different within a row; in each aligned block of 384 rows (0 to 383, 384 to 767, ...) at most 288 rows name the same one
- damping: float32 [4, 3584], P('exp', 'seq'), may hold values from 0.1 to 1
- gate_panel: bfloat16 [4, 3584, 1024], P('exp', 'seq'), may hold values from -6 to 6
Outputs:
- whitened: bfloat16 [4, 3584, 1024], P('exp', 'seq')
The draws below stay inside these ranges and needn't reach their ends.
Inputs may be any that keep to these rules, and one draw needn't show every extreme that they name: `routes`: each token names 2 different experts, and every expert is named by some token. Within the rows of one token shard (aligned blocks of 384 rows) no expert is named by more than 288 rows, a bound that some block reaches.
All inputs are finite; a program needn't handle non-finite values.
Results may differ from the reference program's by a relative error of at most 0.0051.
Values may be sent and summed in bfloat16 or wider, within the bound.
A program may use at most 192 MiB of HBM per device.

```python
import math
import jax
import jax.numpy as jnp
import numpy as np
from jax import lax

D = 3584
FF = 1024
TOPK = 2
TOK_BLK = 384
EXPERTS = 4
CAP = 288
TOKENS = 1536


def shard_levels(stream_key, dims, cuts, least, high):
    gain, own = 1.0, jax.random.fold_in(stream_key, 6)
    for axis_at, shards_of in cuts:
        draws = jnp.exp(jax.random.uniform(jax.random.fold_in(own, axis_at), (shards_of,), jnp.float32, least / len(cuts), high / len(cuts)))
        gain = gain * jnp.repeat(draws, dims[axis_at] // shards_of).reshape([-1 if axis == axis_at else 1 for axis in range(len(dims))])
    return gain


def assign_block(stream_key, own, number, rows, count, top, bound, slope):
    sequence = jax.random.permutation(stream_key, count)
    crowded, common = load_shares(count, rows * top, bound, slope, True), load_shares(count, rows * top, bound, slope, False)
    places = jnp.arange(count)

    def named(sizes, turn):
        used = int((sizes > 0).sum())
        fixed = max(1, used // 4)
        passed = fixed + (places - fixed + turn * (used - fixed)) % max(1, count - fixed)
        return jnp.zeros((count,), jnp.int32).at[sequence[jnp.where(places < fixed, places, passed)]].set(jnp.asarray(sizes, jnp.int32))

    sizes = jnp.where(number % 4 == 0, named(crowded, number // 4), named(common, number - number // 4 - 1))
    mixed = jax.random.permutation(jax.random.fold_in(own, 3), count)
    source_of, sink = mixed[0:count // 2 * 2:2], mixed[1:count // 2 * 2:2]
    slack = jnp.minimum(sizes[source_of] - 1, bound - sizes[sink]) // 2
    slack = jnp.where((source_of == sequence[0]) | (sink == sequence[0]) | (sizes[sink] == 0), 0, jnp.maximum(slack, 0))
    passed = jax.random.randint(jax.random.fold_in(own, 4), (count // 2,), 0, 1 << 20) % (slack + 1)
    sizes = sizes.at[source_of].add(-passed).at[sink].add(passed)
    items = jnp.searchsorted(jnp.cumsum(sizes), jnp.arange(rows * top), side="right").astype(jnp.int32)
    listing = items.reshape(top, rows).T
    listing = listing[jax.random.permutation(jax.random.fold_in(own, 1), rows)]
    turn = jax.random.randint(jax.random.fold_in(own, 2), (rows, 1), 0, top)
    return jnp.take_along_axis(listing, (jnp.arange(top)[None, :] + turn) % top, axis=1)


def load_shares(amount, total, reach, skew, full):
    weights = [(1 << 20) // math.isqrt(standing ** skew) + 1 for standing in range(1, amount + 1)]
    largest = reach if full else min(reach, max(-(-total // amount), total * weights[0] // sum(weights)))
    least = 1 if total - largest >= amount - 1 else 0
    given, spare = [largest] + [least] * (amount - 1), total - largest - least * (amount - 1)
    while spare > 0:
        candidates = [i for i in range(1, amount) if given[i] < largest] or [i for i in range(1, amount) if given[i] < reach]
        pool, remaining = sum([weights[i] for i in candidates]), spare
        for i in candidates:
            extra = min(reach - given[i], max(1, remaining * weights[i] // pool), spare)
            given[i] = given[i] + extra
            spare = spare - extra
    return np.array(given)


def noise(own_key, extent, scale, bound, pieces=(), kind=jnp.bfloat16):
    values = jax.random.normal(own_key, extent, jnp.float32) * scale
    if len(pieces) > 0:
        values = shard_levels(own_key, extent, pieces, -0.22, 0.18) * values
    return jnp.clip(values, min=-bound, max=bound).astype(kind)


def setup_inputs(seed: int = 0) -> dict:
    keys = jax.random.split(jax.random.key(seed), 5)
    tokens = noise(keys[0], (TOKENS, D), 1.0, 6.0, ((0, 4), (1, 8)))
    routes_keys = jax.random.split(jax.random.fold_in(keys[1], 1), TOKENS // TOK_BLK)
    routes_turns = jax.random.permutation(jax.random.fold_in(keys[1], 3), TOKENS // TOK_BLK)
    routes = jax.vmap(lambda own, number: assign_block(jax.random.fold_in(keys[1], 2), own, number, TOK_BLK, EXPERTS, TOPK, CAP, 2))(routes_keys, routes_turns).reshape((TOKENS, TOPK))
    damping = jnp.clip(jnp.exp(math.log(1.0) - 2.3025851 * jax.random.uniform(keys[2], (EXPERTS, D), jnp.float32) ** shard_levels(keys[2], (EXPERTS, D), ((0, 4), (1, 8)), -0.2, 0.2)), 0.1, 1.0)
    gate_panel = noise(keys[3], (EXPERTS, D, FF), 1.0, 6.0, ((0, 4), (1, 8)))
    return {"tokens": tokens, "routes": routes, "damping": damping, "gate_panel": gate_panel}


def reference(tokens, routes, damping, gate_panel):

    def one_expert(index):
        member = jnp.sum((routes == index).astype(jnp.int32), axis=1)
        count = jnp.sum(member).astype(jnp.float32)
        chosen = jnp.where(member[:, None] > 0, tokens, jnp.zeros_like(tokens))
        gram = jnp.dot(chosen.T.astype(jnp.float32), tokens.astype(jnp.float32), preferred_element_type=jnp.float32)
        damp_row = lax.dynamic_index_in_dim(damping, index, 0, keepdims=False)
        hessian = gram / count + jnp.diag(damp_row)
        factor = jnp.linalg.cholesky(hessian)
        weights = lax.dynamic_index_in_dim(gate_panel, index, 0, keepdims=False)
        result = jnp.dot(factor.astype(jnp.bfloat16).T.astype(jnp.float32), weights.astype(jnp.float32), preferred_element_type=jnp.float32)
        return result.astype(jnp.bfloat16)
    return lax.map(one_expert, jnp.arange(EXPERTS, dtype=jnp.int32))
```

```python
import functools

import jax
import jax.numpy as jnp
from jax import lax
from jax.experimental import pallas as pl
from jax.experimental.pallas import tpu as pltpu
from jax.sharding import PartitionSpec as P

TILE = 256
HALF = 128
CHUNK = 4
NT = (((1,), (1,)), ((), ()))
NN = (((1,), (0,)), ((), ()))
F32 = jnp.float32
BF16 = jnp.bfloat16


def split(value):
    high = value.astype(BF16)
    return high, (value - high.astype(F32)).astype(BF16)


def mm(a, b, dims):
    return lax.dot_general(a, b, dims, preferred_element_type=F32)


def mm3(a, b, dims):
    ah, al = split(a)
    bh, bl = split(b)
    return mm(ah, bh, dims) + (mm(al, bh, dims) + mm(ah, bl, dims))


def factor_half(block):
    rows = lax.broadcasted_iota(jnp.int32, (8, HALF), 0)
    lanes = lax.broadcasted_iota(jnp.int32, (8, HALF), 1)
    count = HALF // 8
    left = [block[8 * t:8 * t + 8, :] for t in range(count)]
    right = [jnp.where(lanes == rows + 8 * t, 1.0, 0.0).astype(F32) for t in range(count)]
    for p in range(count):
        pl_, pr_ = left[p], right[p]
        cols = [jnp.broadcast_to(pl_[:, 8 * p + k:8 * p + k + 1], (8, HALF)) for k in range(8)]
        for k in range(8):
            scale = lax.rsqrt(cols[k][k:k + 1, :])
            lcol = cols[k] * scale
            ul = pl_[k:k + 1, :] * scale
            ur = pr_[k:k + 1, :] * scale
            for j in range(k + 1, 8):
                cols[j] = cols[j] - lcol * lcol[j:j + 1, :]
            below = jnp.where(rows > k, lcol, 0.0)
            pl_ = jnp.where(rows == k, ul, pl_ - below * ul)
            pr_ = jnp.where(rows == k, ur, pr_ - below * ur)
        left[p] = jnp.where(lanes >= rows + 8 * p, pl_, 0.0)
        right[p] = pr_
        if p + 1 < count:
            both = jnp.concatenate([left[p], pr_], axis=1)
            high = both.astype(BF16).astype(F32)
            low = both - high
            lhs = jnp.concatenate([high[:, :HALF], low[:, :HALF], high[:, :HALF]], axis=0)
            rhs = jnp.concatenate([high, high, low], axis=0).astype(BF16)
            update = mm(lhs.T.astype(BF16), rhs, NN)
            for t in range(p + 1, count):
                left[t] = left[t] - update[8 * t:8 * t + 8, :HALF]
                right[t] = right[t] - update[8 * t:8 * t + 8, HALF:]
    return jnp.concatenate(left, axis=0), jnp.concatenate(right, axis=0)


def factor_kernel(tiles, own_tiles, block_width, xt, damp, inv_count, out, hi, lo, acc, half, lower, inv, l21, wh, wl, sem):
    first_own = lax.axis_index("seq") * block_width // TILE

    def offset(j):
        return j * tiles - (j * (j - 1)) // 2

    def column(j, carry):
        chunks = (tiles - j + CHUNK - 1) // CHUNK
        own_x = pl.ds(pl.multiple_of(j * TILE, TILE), TILE)

        def chunk(c, inner):
            i0 = j + c * CHUNK
            for r in range(CHUNK):
                xr = jnp.minimum(i0 + r, tiles - 1)
                acc[pl.ds(r * TILE, TILE), :] = (
                    mm(xt[pl.ds(pl.multiple_of(xr * TILE, TILE), TILE), :], xt[own_x, :], NT) * inv_count[0, 0]
                )

            def earlier(k, z):
                base = offset(k)
                ah = hi[pl.ds(base + i0 - k, CHUNK)].reshape(CHUNK * TILE, TILE)
                al = lo[pl.ds(base + i0 - k, CHUNK)].reshape(CHUNK * TILE, TILE)
                bh, bl = hi[base + j - k], lo[base + j - k]
                acc[...] -= mm(ah, bh, NT) + (mm(al, bh, NT) + mm(ah, bl, NT))
                return z

            lax.fori_loop(0, j, earlier, 0)

            @pl.when(c == 0)
            def _():
                rows = lax.broadcasted_iota(jnp.int32, (TILE, TILE), 0)
                lanes = lax.broadcasted_iota(jnp.int32, (TILE, TILE), 1)
                acc[pl.ds(0, TILE), :] += jnp.where(rows == lanes, damp[j], 0.0)
                half[0] = acc[pl.ds(0, HALF), pl.ds(0, HALF)]

                def one(h, z):
                    upper, inverse = factor_half(half[h])
                    lower[h] = upper.T
                    inv[h] = inverse

                    @pl.when(h == 0)
                    def _():
                        cross = mm3(acc[pl.ds(HALF, HALF), pl.ds(0, HALF)], inverse, NT)
                        l21[...] = cross
                        half[1] = acc[pl.ds(HALF, HALF), pl.ds(HALF, HALF)] - mm3(cross, cross, NT)

                    return z

                lax.fori_loop(0, 2, one, 0)
                corner = -mm3(mm3(inv[1], l21[...], NN), inv[0], NN)
                zeros = jnp.zeros((HALF, HALF), F32)
                whole = jnp.concatenate(
                    [jnp.concatenate([inv[0], zeros], axis=1), jnp.concatenate([corner, inv[1]], axis=1)], axis=0
                )
                wh[...], wl[...] = split(whole)

            sh, sl = split(acc[...])
            solved = mm(sh, wh[...], NT) + (mm(sl, wh[...], NT) + mm(sh, wl[...], NT))
            top, rest = split(solved)
            at = pl.ds(offset(j) + c * CHUNK, CHUNK)
            hi[at] = top.reshape(CHUNK, TILE, TILE)
            lo[at] = rest.reshape(CHUNK, TILE, TILE)

            @pl.when(c == 0)
            def _():
                zeros = jnp.zeros((HALF, HALF), F32)
                whole = jnp.concatenate(
                    [jnp.concatenate([lower[0], zeros], axis=1), jnp.concatenate([l21[...], lower[1]], axis=1)], axis=0
                )
                hi[offset(j)], lo[offset(j)] = split(whole)

            return inner

        lax.fori_loop(0, chunks, chunk, 0)
        mine = j - first_own

        @pl.when((mine >= 0) & (mine < own_tiles))
        def _():
            copy = pltpu.make_async_copy(hi.at[pl.ds(offset(j), tiles)], out.at[mine, pl.ds(j, tiles)], sem)
            copy.start()
            copy.wait()

        return carry

    lax.fori_loop(0, tiles, column, 0)


def factor_columns(xt, damp, inv_count, block_width):
    total_rows, depth = xt.shape
    tiles = total_rows // TILE
    own_tiles = (block_width - 1 + TILE - 1) // TILE + 1
    room = tiles * (tiles + 1) // 2 + tiles
    vmem = pl.BlockSpec(memory_space=pltpu.VMEM)
    out = pl.pallas_call(
        functools.partial(factor_kernel, tiles, own_tiles, block_width),
        out_shape=jax.ShapeDtypeStruct((own_tiles, 2 * tiles, TILE, TILE), BF16),
        in_specs=[vmem, vmem, pl.BlockSpec(memory_space=pltpu.SMEM)],
        out_specs=pl.BlockSpec(memory_space=pl.ANY),
        scratch_shapes=[
            pltpu.VMEM((room, TILE, TILE), BF16),
            pltpu.VMEM((room, TILE, TILE), BF16),
            pltpu.VMEM((CHUNK * TILE, TILE), F32),
            pltpu.VMEM((2, HALF, HALF), F32),
            pltpu.VMEM((2, HALF, HALF), F32),
            pltpu.VMEM((2, HALF, HALF), F32),
            pltpu.VMEM((HALF, HALF), F32),
            pltpu.VMEM((TILE, TILE), BF16),
            pltpu.VMEM((TILE, TILE), BF16),
            pltpu.SemaphoreType.DMA,
        ],
        compiler_params=pltpu.CompilerParams(vmem_limit_bytes=56 * 1024 * 1024),
        cost_estimate=pl.CostEstimate(
            flops=2 * total_rows**3 + total_rows * total_rows * depth,
            bytes_accessed=2 * total_rows * (depth + own_tiles * TILE),
            transcendentals=total_rows,
        ),
    )(xt, damp.reshape(tiles, 1, TILE), inv_count.reshape(1, 1))
    return out


def per_device(tokens, routes, damping, gate_panel):
    seq_count = lax.axis_size("seq")
    exp_count = lax.axis_size("exp")
    seq_index = lax.axis_index("seq")
    exp_index = lax.axis_index("exp")
    tok_rows, block_width = tokens.shape
    top_count = routes.shape[1]
    capacity = tok_rows * top_count * 3 // (2 * exp_count)
    total_rows = block_width * seq_count
    experts = jnp.arange(exp_count, dtype=jnp.int32)
    named = jnp.any(routes[:, :, None] == experts[None, None, :], axis=1).astype(jnp.int32)
    slot = jnp.where(named > 0, jnp.cumsum(named, axis=0) - named, capacity)
    dispatch = (slot.T[:, :, None] == jnp.arange(capacity, dtype=jnp.int32)[None, None, :]).astype(BF16)
    counts = lax.psum(jnp.sum(named, axis=0).astype(F32), "exp")
    own_count = jnp.sum(jnp.where(experts == exp_index, counts, 0.0))
    outgoing = lax.dot_general(
        jnp.broadcast_to(tokens[None], (exp_count, tok_rows, block_width)), dispatch,
        (((1,), (1,)), ((0,), (0,))), preferred_element_type=F32
    ).astype(BF16)
    arrived = lax.all_to_all(outgoing, "exp", split_axis=0, concat_axis=0, tiled=True)
    own_xt = jnp.transpose(arrived, (1, 0, 2)).reshape(block_width, exp_count * capacity)
    xt = lax.all_gather(own_xt, "seq", axis=0, tiled=True)
    damp = lax.all_gather(damping[0], "seq", axis=0, tiled=True)
    panel = lax.all_gather(gate_panel[0], "seq", axis=0, tiled=True)
    out = factor_columns(xt, damp, 1.0 / own_count, block_width)
    own_tiles, tiles = out.shape[0], total_rows // TILE
    start = seq_index * block_width
    first = start // TILE * TILE
    columns = jnp.transpose(out[:, :tiles].reshape(own_tiles, total_rows, TILE), (1, 0, 2))
    columns = columns.reshape(total_rows, own_tiles * TILE)
    columns = lax.dynamic_slice_in_dim(columns, start - first, block_width, 1)
    row_ids = jnp.arange(total_rows, dtype=jnp.int32)[:, None]
    col_ids = jnp.arange(block_width, dtype=jnp.int32)[None, :] + start
    factor_b = jnp.where(row_ids >= col_ids, columns, jnp.zeros_like(columns))
    result = lax.dot_general(factor_b, panel, (((0,), (0,)), ((), ())), preferred_element_type=F32)
    return result.astype(BF16)[None]


def solution(mesh):
    in_specs = (P("exp", "seq"), P("exp", None), P("exp", "seq"), P("exp", "seq", None))
    out_specs = P("exp", "seq", None)
    return jax.shard_map(
        per_device, mesh=mesh, in_specs=in_specs, out_specs=out_specs, check_vma=False
    )
```

```python
import functools

import jax
import jax.numpy as jnp
from jax import lax
from jax.experimental import pallas as pl
from jax.experimental.pallas import tpu as pltpu
from jax.sharding import PartitionSpec as P

TILE = 256
HALF = 128
CHUNK = 4
NT = (((1,), (1,)), ((), ()))
NN = (((1,), (0,)), ((), ()))
F32 = jnp.float32
BF16 = jnp.bfloat16


def split(value):
    high = value.astype(BF16)
    return high, (value - high.astype(F32)).astype(BF16)


def mm(a, b, dims):
    return lax.dot_general(a, b, dims, preferred_element_type=F32)


def mm3(a, b, dims):
    ah, al = split(a)
    bh, bl = split(b)
    return mm(ah, bh, dims) + (mm(al, bh, dims) + mm(ah, bl, dims))


def factor_half(block):
    rows = lax.broadcasted_iota(jnp.int32, (8, HALF), 0)
    lanes = lax.broadcasted_iota(jnp.int32, (8, HALF), 1)
    count = HALF // 8
    left = [block[8 * t:8 * t + 8, :] for t in range(count)]
    right = [jnp.where(lanes == rows + 8 * t, 1.0, 0.0).astype(F32) for t in range(count)]
    for p in range(count):
        pl_, pr_ = left[p], right[p]
        cols = [jnp.broadcast_to(pl_[:, 8 * p + k:8 * p + k + 1], (8, HALF)) for k in range(8)]
        for k in range(8):
            scale = lax.rsqrt(cols[k][k:k + 1, :])
            lcol = cols[k] * scale
            ul = pl_[k:k + 1, :] * scale
            ur = pr_[k:k + 1, :] * scale
            for j in range(k + 1, 8):
                cols[j] = cols[j] - lcol * lcol[j:j + 1, :]
            below = jnp.where(rows > k, lcol, 0.0)
            pl_ = jnp.where(rows == k, ul, pl_ - below * ul)
            pr_ = jnp.where(rows == k, ur, pr_ - below * ur)
        left[p] = jnp.where(lanes >= rows + 8 * p, pl_, 0.0)
        right[p] = pr_
        if p + 1 < count:
            both = jnp.concatenate([left[p], pr_], axis=1)
            high = both.astype(BF16).astype(F32)
            low = both - high
            lhs = jnp.concatenate([high[:, :HALF], low[:, :HALF], high[:, :HALF]], axis=0)
            rhs = jnp.concatenate([high, high, low], axis=0).astype(BF16)
            update = mm(lhs.T.astype(BF16), rhs, NN)
            for t in range(p + 1, count):
                left[t] = left[t] - update[8 * t:8 * t + 8, :HALF]
                right[t] = right[t] - update[8 * t:8 * t + 8, HALF:]
    return jnp.concatenate(left, axis=0), jnp.concatenate(right, axis=0)


def factor_kernel(tiles, own_tiles, block_width, xt, damp, inv_count, out, hi, lo, acc, half, lower, inv, l21, wh, wl, sem):
    first_own = lax.axis_index("seq") * block_width // TILE

    def offset(j):
        return j * tiles - (j * (j - 1)) // 2

    def column(j, carry):
        chunks = (tiles - j + CHUNK - 1) // CHUNK
        own_x = pl.ds(pl.multiple_of(j * TILE, TILE), TILE)

        def chunk(c, inner):
            i0 = j + c * CHUNK
            for r in range(CHUNK):
                xr = jnp.minimum(i0 + r, tiles - 1)
                acc[pl.ds(r * TILE, TILE), :] = (
                    mm(xt[pl.ds(pl.multiple_of(xr * TILE, TILE), TILE), :], xt[own_x, :], NT) * inv_count[0, 0]
                )

            def earlier(k, z):
                base = offset(k)
                ah = hi[pl.ds(base + i0 - k, CHUNK)].reshape(CHUNK * TILE, TILE)
                al = lo[pl.ds(base + i0 - k, CHUNK)].reshape(CHUNK * TILE, TILE)
                bh, bl = hi[base + j - k], lo[base + j - k]
                acc[...] -= mm(ah, bh, NT) + (mm(al, bh, NT) + mm(ah, bl, NT))
                return z

            lax.fori_loop(0, j, earlier, 0)

            @pl.when(c == 0)
            def _():
                rows = lax.broadcasted_iota(jnp.int32, (TILE, TILE), 0)
                lanes = lax.broadcasted_iota(jnp.int32, (TILE, TILE), 1)
                acc[pl.ds(0, TILE), :] += jnp.where(rows == lanes, damp[j], 0.0)
                half[0] = acc[pl.ds(0, HALF), pl.ds(0, HALF)]

                def one(h, z):
                    upper, inverse = factor_half(half[h])
                    lower[h] = upper.T
                    inv[h] = inverse

                    @pl.when(h == 0)
                    def _():
                        cross = mm3(acc[pl.ds(HALF, HALF), pl.ds(0, HALF)], inverse, NT)
                        l21[...] = cross
                        half[1] = acc[pl.ds(HALF, HALF), pl.ds(HALF, HALF)] - mm3(cross, cross, NT)

                    return z

                lax.fori_loop(0, 2, one, 0)
                corner = -mm3(mm3(inv[1], l21[...], NN), inv[0], NN)
                zeros = jnp.zeros((HALF, HALF), F32)
                whole = jnp.concatenate(
                    [jnp.concatenate([inv[0], zeros], axis=1), jnp.concatenate([corner, inv[1]], axis=1)], axis=0
                )
                wh[...], wl[...] = split(whole)

            sh, sl = split(acc[...])
            solved = mm(sh, wh[...], NT) + (mm(sl, wh[...], NT) + mm(sh, wl[...], NT))
            top, rest = split(solved)
            at = pl.ds(offset(j) + c * CHUNK, CHUNK)
            hi[at] = top.reshape(CHUNK, TILE, TILE)
            lo[at] = rest.reshape(CHUNK, TILE, TILE)

            @pl.when(c == 0)
            def _():
                zeros = jnp.zeros((HALF, HALF), F32)
                whole = jnp.concatenate(
                    [jnp.concatenate([lower[0], zeros], axis=1), jnp.concatenate([l21[...], lower[1]], axis=1)], axis=0
                )
                hi[offset(j)], lo[offset(j)] = split(whole)

            return inner

        lax.fori_loop(0, chunks, chunk, 0)
        mine = j - first_own

        @pl.when((mine >= 0) & (mine < own_tiles))
        def _():
            own_copy(j, mine).start()

        return carry

    def own_copy(j, mine):
        return pltpu.make_async_copy(
            hi.at[pl.ds(offset(j) - j, tiles)],
            out.at[:, :, pl.ds(pl.multiple_of(mine * TILE, TILE), TILE)],
            sem.at[mine],
        )

    lax.fori_loop(0, tiles, column, 0)
    for mine in range(own_tiles):

        @pl.when(first_own + mine < tiles)
        def _(mine=mine):
            own_copy(first_own + mine, mine).wait()


def factor_columns(xt, damp, inv_count, block_width):
    total_rows, depth = xt.shape
    tiles = total_rows // TILE
    own_tiles = (block_width - 1 + TILE - 1) // TILE + 1
    room = tiles * (tiles + 1) // 2 + tiles
    vmem = pl.BlockSpec(memory_space=pltpu.VMEM)
    out = pl.pallas_call(
        functools.partial(factor_kernel, tiles, own_tiles, block_width),
        out_shape=jax.ShapeDtypeStruct((tiles, TILE, own_tiles * TILE), BF16),
        in_specs=[vmem, vmem, pl.BlockSpec(memory_space=pltpu.SMEM)],
        out_specs=pl.BlockSpec(memory_space=pl.ANY),
        scratch_shapes=[
            pltpu.VMEM((room, TILE, TILE), BF16),
            pltpu.VMEM((room, TILE, TILE), BF16),
            pltpu.VMEM((CHUNK * TILE, TILE), F32),
            pltpu.VMEM((2, HALF, HALF), F32),
            pltpu.VMEM((2, HALF, HALF), F32),
            pltpu.VMEM((2, HALF, HALF), F32),
            pltpu.VMEM((HALF, HALF), F32),
            pltpu.VMEM((TILE, TILE), BF16),
            pltpu.VMEM((TILE, TILE), BF16),
            pltpu.SemaphoreType.DMA((own_tiles,)),
        ],
        compiler_params=pltpu.CompilerParams(vmem_limit_bytes=56 * 1024 * 1024),
        cost_estimate=pl.CostEstimate(
            flops=2 * total_rows**3 + total_rows * total_rows * depth,
            bytes_accessed=2 * total_rows * (depth + own_tiles * TILE),
            transcendentals=total_rows,
        ),
    )(xt, damp.reshape(tiles, 1, TILE), inv_count.reshape(1, 1))
    return out


def per_device(tokens, routes, damping, gate_panel):
    seq_count = lax.axis_size("seq")
    exp_count = lax.axis_size("exp")
    seq_index = lax.axis_index("seq")
    exp_index = lax.axis_index("exp")
    tok_rows, block_width = tokens.shape
    top_count = routes.shape[1]
    capacity = tok_rows * top_count * 3 // (2 * exp_count)
    total_rows = block_width * seq_count
    experts = jnp.arange(exp_count, dtype=jnp.int32)
    named = jnp.any(routes[:, :, None] == experts[None, None, :], axis=1).astype(jnp.int32)
    slot = jnp.where(named > 0, jnp.cumsum(named, axis=0) - named, capacity)
    dispatch = (slot.T[:, :, None] == jnp.arange(capacity, dtype=jnp.int32)[None, None, :]).astype(BF16)
    counts = lax.psum(jnp.sum(named, axis=0).astype(F32), "exp")
    own_count = jnp.sum(jnp.where(experts == exp_index, counts, 0.0))
    outgoing = lax.dot_general(
        jnp.broadcast_to(tokens[None], (exp_count, tok_rows, block_width)), dispatch,
        (((1,), (1,)), ((0,), (0,))), preferred_element_type=F32
    ).astype(BF16)
    arrived = lax.all_to_all(outgoing, "exp", split_axis=0, concat_axis=0, tiled=True)
    own_xt = jnp.transpose(arrived, (1, 0, 2)).reshape(block_width, exp_count * capacity)
    xt = lax.all_gather(own_xt, "seq", axis=0, tiled=True)
    damp = lax.all_gather(damping[0], "seq", axis=0, tiled=True)
    panel = lax.all_gather(gate_panel[0], "seq", axis=0, tiled=True)
    out = factor_columns(xt, damp, 1.0 / own_count, block_width)
    columns = out.reshape(total_rows, out.shape[2])
    start = seq_index * block_width
    first = start // TILE * TILE
    row_ids = jnp.arange(total_rows, dtype=jnp.int32)[:, None]
    col_ids = jnp.arange(columns.shape[1], dtype=jnp.int32)[None, :] + first
    factor_b = jnp.where(row_ids >= col_ids, columns, jnp.zeros_like(columns))
    result = lax.dot_general(factor_b, panel, (((0,), (0,)), ((), ())), preferred_element_type=F32)
    return lax.dynamic_slice_in_dim(result.astype(BF16), start - first, block_width, 0)[None]


def solution(mesh):
    in_specs = (P("exp", "seq"), P("exp", None), P("exp", "seq"), P("exp", "seq", None))
    out_specs = P("exp", "seq", None)
    return jax.shard_map(
        per_device, mesh=mesh, in_specs=in_specs, out_specs=out_specs, check_vma=False
    )
```
